1024 devices in a mesh: sub: 64 (over z, core), dom: 16 (over x, y).
Axes of the slice: x: 4, y: 4, z: 32, core: 2. Of those that a mesh axis runs over, the one named last changes fastest.
Arguments:
- a_cols: int32 [3072, 27], P(('sub', 'dom')), may hold values from 0 to 24, as said below
- a_blocks: bfloat16 [3072, 27, 128, 128], P(('sub', 'dom')), may hold values from -0.5 to 0.5
- p_blocks: bfloat16 [3072, 128, 128], P(('sub', 'dom')), may hold values from -1.1953125 to 1.1953125
- send_rows: int32 [16384, 1], P(('sub', 'dom')), may hold values from -1 to 2, as said below
Outputs:
- coarse: bfloat16 [1024, 128, 2304], P(('sub', 'dom'))
The draws below stay inside these ranges and needn't reach their ends.
Inputs may be any that keep to these rules, and one draw needn't show every extreme that they name: a_cols[i, 0] is 3 + i % 3 (the row itself). Codes below 3 occur only for subdomains s > 0, codes from 6 to 8 only for s < 63. A code 3 * 3 + p + m has p != d and names a slot m that holds a row in the list of device (s, p) to device (s, d). Codes may repeat within a row; repeated blocks add. `send_rows`: entry (s * 16 + p) * 16 + d lists distinct rows of device (s, p) for device (s, d), then -1; the list of a device to itself is all -1. Every listed row is named by some code of the receiving device. In every draw and every subdomain some pair holds 1 row; the number per pair is uneven, some receivers get 1 from every peer.
All inputs are finite; a program needn't handle non-finite values.
Results may differ from the reference program's by a relative error of at most 0.0049.
Values may be sent and summed in bfloat16 or wider, within the bound.
A program may use at most 32 MiB of HBM per device.

```python
import jax
import jax.numpy as jnp
from jax import lax

B = 128
KA = 27
CA = 1
R = 3
CAP = 1
NF = 3072
N_SUB = 64
N_DOM = 16


def pattern_layout(key):
    devices = N_SUB * N_DOM
    subkeys = jax.random.split(key, 4)
    base_count = jax.random.randint(subkeys[0], (N_SUB, N_DOM, N_DOM), 0, CAP + 1)
    heavy_recv = jax.random.randint(subkeys[1], (N_SUB, N_DOM, 1), 0, 4) == 0
    counts = jnp.where(heavy_recv, CAP, base_count)
    receiver = jnp.arange(N_DOM)[:, None]
    sender = jnp.arange(N_DOM)[None, :]
    counts = jnp.where(sender == (receiver + 1) % N_DOM, CAP, counts)
    counts = jnp.where(sender == receiver, 0, counts)
    scores = jax.random.randint(subkeys[2], (N_SUB, N_DOM, N_DOM, R), 0, 1 << 20) * R + jnp.arange(R)
    ordering = jnp.argsort(scores, axis=-1)
    picked = ordering[..., :CAP]
    usable = jnp.arange(CAP)[None, None, None, :] < counts[..., None]
    listed = jnp.where(usable, picked, -1).astype(jnp.int32)
    send_rows = jnp.transpose(listed, (0, 2, 1, 3)).reshape(devices * N_DOM, CAP)
    near_count = 3 * R
    code_total = near_count + N_DOM * CAP
    sub_place = jnp.arange(devices) // N_DOM
    code_range = jnp.arange(near_count)
    lower_ok = (code_range < R)[None, :] & (sub_place > 0)[:, None]
    own_ok = jnp.broadcast_to(((code_range >= R) & (code_range < 2 * R))[None, :], (devices, near_count))
    upper_ok = (code_range >= 2 * R)[None, :] & (sub_place < N_SUB - 1)[:, None]
    remote_valid = usable.reshape(devices, N_DOM * CAP)
    allowed = jnp.concatenate([lower_ok | own_ok | upper_ok, remote_valid], axis=1)
    free_slots = R * (KA - 1)
    remote_rank = jnp.cumsum(remote_valid.astype(jnp.int32), axis=1) - 1
    remote_total = jnp.sum(remote_valid.astype(jnp.int32), axis=1)
    position = jnp.arange(free_slots)
    remote_codes = near_count + jnp.arange(N_DOM * CAP)
    matches = remote_valid[:, None, :] & (remote_rank[:, None, :] == position[None, :, None])
    covered = jnp.sum(jnp.where(matches, remote_codes[None, None, :], 0), axis=2)
    usable_count = jnp.sum(allowed.astype(jnp.int32), axis=1)
    random_pick = jax.random.randint(subkeys[3], (devices, free_slots), 0, 1 << 20) % usable_count[:, None]
    allowed_rank = jnp.cumsum(allowed.astype(jnp.int32), axis=1) - 1
    chosen_hit = allowed[:, None, :] & (allowed_rank[:, None, :] == random_pick[:, :, None])
    chosen = jnp.sum(jnp.where(chosen_hit, jnp.arange(code_total)[None, None, :], 0), axis=2)
    filled = jnp.where(position[None, :] < remote_total[:, None], covered, chosen)
    filled = jnp.transpose(filled.reshape(devices, KA - 1, R), (0, 2, 1))
    own_codes = jnp.broadcast_to((R + jnp.arange(R))[None, :, None], (devices, R, 1))
    a_cols = jnp.concatenate([own_codes, filled], axis=2).reshape(devices * R, KA).astype(jnp.int32)
    return (a_cols, send_rows)


def draw_a_cols(key, part):
    layout = pattern_layout(jax.random.fold_in(key, 11))
    return layout[0]


def draw_send_rows(key, part):
    layout = pattern_layout(jax.random.fold_in(key, 11))
    return layout[1]


def levels(key, dims, cuts, low, largest):
    def one(dim, parts):
        draws = jax.random.uniform(jax.random.fold_in(jax.random.fold_in(key, 6), dim), (parts,), jnp.float32, low / len(cuts), largest / len(cuts))
        return jnp.repeat(jnp.exp(draws), dims[dim] // parts).reshape((-1,) + (1,) * (len(dims) - dim - 1))

    factor_of = one(*cuts[0])
    for cut in cuts[1:]:
        factor_of = factor_of * one(*cut)
    return factor_of


def normal_values(key, extent, spread, bound, pieces=(), kind=jnp.bfloat16):
    entries = jax.random.normal(key, extent, jnp.float32) * spread
    if len(pieces) > 0:
        entries = levels(key, extent, pieces, -0.22, 0.18) * entries
    return jnp.clip(entries, min=-bound, max=bound).astype(kind)


def setup_inputs(seed: int = 0) -> dict:
    key_of = jax.random.split(jax.random.key(seed), 5)
    a_cols = draw_a_cols(jax.random.fold_in(key_of[4], 71), 0)
    a_blocks = normal_values(key_of[1], (NF, KA, B, B), B ** -0.5, 0.5, ((0, 1024),))
    p_blocks = normal_values(key_of[2], (NF, B, CA * B), 0.2, 1.1953125, ((0, 1024),))
    send_rows = draw_send_rows(jax.random.fold_in(key_of[4], 71), 0)
    return {"a_cols": a_cols, "a_blocks": a_blocks, "p_blocks": p_blocks, "send_rows": send_rows}


def device_coarse(device, a_cols, a_blocks, p_blocks, send_rows):
    sub_place = device // N_DOM
    dom_place = device % N_DOM
    flat_codes = lax.dynamic_slice_in_dim(a_cols, (device * R).astype(jnp.int32), R, 0).reshape(-1)
    a_local = lax.dynamic_slice_in_dim(a_blocks, (device * R).astype(jnp.int32), R, 0)
    p_local = lax.dynamic_slice_in_dim(p_blocks, (device * R).astype(jnp.int32), R, 0)
    near_count = 3 * R
    remote_index = jnp.clip(flat_codes - near_count, 0, N_DOM * CAP - 1)
    source_peer = remote_index // CAP
    peer_slot = remote_index % CAP
    sub_lists = lax.dynamic_slice_in_dim(send_rows, (sub_place * N_DOM * N_DOM).astype(jnp.int32), N_DOM * N_DOM, 0)
    listed_row = sub_lists[source_peer * N_DOM + dom_place, peer_slot]
    source_row = jnp.where(
        flat_codes < R,
        ((sub_place - 1) * N_DOM + dom_place) * R + flat_codes,
        jnp.where(
            flat_codes < 2 * R,
            device * R + flat_codes - R,
            jnp.where(
                flat_codes < near_count,
                ((sub_place + 1) * N_DOM + dom_place) * R + flat_codes - 2 * R,
                (sub_place * N_DOM + source_peer) * R + listed_row,
            ),
        ),
    )
    source_row = jnp.clip(source_row, 0, R * N_SUB * N_DOM - 1).astype(jnp.int32)
    picked = jnp.take(p_blocks, source_row, axis=0)
    products = jnp.einsum(
        "nab,nbc->nac",
        a_local.reshape(R * KA, B, B).astype(jnp.float32),
        picked.astype(jnp.float32),
        precision=lax.Precision.HIGHEST,
    )
    window_group = jnp.where(
        flat_codes < R,
        N_DOM,
        jnp.where(flat_codes < 2 * R, dom_place, jnp.where(flat_codes < near_count, N_DOM + 1, source_peer)),
    )
    member = (window_group[:, None] == jnp.arange(N_DOM + 2)[None, :]).astype(jnp.float32)
    member = member.reshape(R, KA, N_DOM + 2)
    summed = jnp.einsum(
        "rkt,rkbc->rtbc",
        member,
        products.reshape(R, KA, B, CA * B),
        precision=lax.Precision.HIGHEST,
    )
    fine_coarse = jnp.transpose(summed, (0, 2, 1, 3)).reshape(R, B, (N_DOM + 2) * CA * B).astype(jnp.bfloat16)
    coarse = jnp.dot(
        p_local.reshape(R * B, CA * B).T,
        fine_coarse.reshape(R * B, (N_DOM + 2) * CA * B),
        preferred_element_type=jnp.float32,
    )
    return coarse.reshape(CA, B, (N_DOM + 2) * CA * B).astype(jnp.bfloat16)


def reference(a_cols, a_blocks, p_blocks, send_rows):
    devices = jnp.arange(N_SUB * N_DOM, dtype=jnp.int32)
    result = lax.map(lambda device: device_coarse(device, a_cols, a_blocks, p_blocks, send_rows), devices)
    return result.reshape(CA * N_SUB * N_DOM, B, (N_DOM + 2) * CA * B)
```

```python
import functools

import jax
import jax.numpy as jnp
from jax import lax
from jax.experimental import pallas as pl
from jax.experimental.pallas import tpu as pltpu
from jax.sharding import PartitionSpec as P

MESH = pl.DeviceIdType.MESH
F32 = jnp.float32
BF16 = jnp.bfloat16


def kernel(
    n_sub, n_dom, rows, per_row, size,
    cols, send_rows, a_hbm, p_hbm, out,
    a_buf, p_buf, stage, far, near, part, pairs, table, links,
    a_sem, p_sem, link_sem, far_send, far_recv, near_send, near_recv,
):
    sub, dom = lax.axis_index("sub"), lax.axis_index("dom")
    above, below = lax.rem(sub + 1, n_sub), lax.rem(sub + n_sub - 1, n_sub)
    items = rows * per_row
    codes = 3 * rows + n_dom

    barrier = pltpu.get_barrier_semaphore()
    for step in range(1, n_dom):
        peer = lax.rem(dom + step, n_dom)
        pl.semaphore_signal(barrier, inc=1, device_id={"dom": peer}, device_id_type=MESH)
    for other in (above, below):
        pl.semaphore_signal(barrier, inc=1, device_id={"sub": other}, device_id_type=MESH)

    p_copy = pltpu.make_async_copy(p_hbm, p_buf, p_sem)
    p_copy.start()
    a_copies = [
        pltpu.make_async_copy(a_hbm.at[r], a_buf.at[r], a_sem.at[r]) for r in range(rows)
    ]
    for copy in a_copies:
        copy.start()

    lane = lax.broadcasted_iota(jnp.int32, (1, 128), 1)
    last = jnp.full((1, 128), items, jnp.int32)
    for j in range(items):
        table[pl.ds(j, 1), :] = last
        last = jnp.where(lane == cols[j // per_row, j % per_row], j, last)
    table[pl.ds(items, 1), :] = last
    link_copy = pltpu.make_async_copy(table, links, link_sem)
    link_copy.start()

    p_copy.wait()
    for step in range(1, n_dom):
        peer = lax.rem(dom + step, n_dom)
        row = jnp.clip(send_rows[peer], 0, rows - 1)
        stage[step] = p_buf[row]

    pl.semaphore_wait(barrier, n_dom + 1)
    far_copies = []
    for step in range(1, n_dom):
        peer = lax.rem(dom + step, n_dom)
        far_copies.append(
            pltpu.make_async_remote_copy(
                src_ref=stage.at[step], dst_ref=far.at[step],
                send_sem=far_send.at[step], recv_sem=far_recv.at[step],
                device_id={"dom": peer}, device_id_type=MESH,
            )
        )
        far_copies[-1].start()
    near_copies = []
    for place, other in ((0, above), (1, below)):
        near_copies.append(
            pltpu.make_async_remote_copy(
                src_ref=p_buf, dst_ref=near.at[place],
                send_sem=near_send.at[place], recv_sem=near_recv.at[place],
                device_id={"sub": other}, device_id_type=MESH,
            )
        )
        near_copies[-1].start()

    for r in range(rows):
        left = p_buf[r].T
        a_copies[r].wait()
        group = next(g for g in (9, 8, 6, 5, 4, 3, 2, 1) if per_row % g == 0)

        @pl.loop(0, per_row // group)
        def _(block):
            base = block * group
            for k in range(group):
                part[r * per_row + base + k] = jnp.dot(
                    left, a_buf[r, base + k], preferred_element_type=F32
                )

    part[items] = jnp.zeros((size, size), F32)
    link_copy.wait()
    for r in range(rows):

        @pl.loop(0, per_row)
        def _(k):
            j = r * per_row + k
            part[j] += part[links[j, cols[r, k]]]

    @pl.loop(0, codes)
    def _(v):
        total = part[links[items, v]]
        high = total.astype(BF16)
        low = (total - high.astype(F32)).astype(BF16)
        pairs[v] = jnp.concatenate([high, low], axis=1)

    def window(first, blocks):
        left = jnp.concatenate([pairs[first + i] for i in range(len(blocks))], axis=1)
        right = jnp.concatenate([b for b in blocks for _ in range(2)], axis=0)
        return jnp.dot(left, right, preferred_element_type=F32).astype(BF16)

    def put(place, value):
        out[0, :, pl.ds(pl.multiple_of(place * size, size), size)] = value

    put(dom, window(rows, [p_buf[r] for r in range(rows)]))
    for place in range(2):
        near_copies[place].wait()
        put(n_dom + place, window(2 * rows * place, [near[place, r] for r in range(rows)]))
    for step in range(1, n_dom):
        far_copies[step - 1].wait()
        source = lax.rem(dom + n_dom - step, n_dom)
        put(source, window(3 * rows + source, [far[step]]))


def per_device(n_sub, n_dom, a_cols, a_blocks, p_blocks, send_rows):
    rows, per_row = a_cols.shape
    size = p_blocks.shape[1]
    items = rows * per_row
    table_rows = (items + 8) // 8 * 8
    block = (size, size)
    dma = pltpu.SemaphoreType.DMA
    return pl.pallas_call(
        functools.partial(kernel, n_sub, n_dom, rows, per_row, size),
        out_shape=jax.ShapeDtypeStruct((1, size, (n_dom + 2) * size), BF16),
        in_specs=[
            pl.BlockSpec(memory_space=pltpu.SMEM),
            pl.BlockSpec(memory_space=pltpu.SMEM),
            pl.BlockSpec(memory_space=pltpu.HBM),
            pl.BlockSpec(memory_space=pltpu.HBM),
        ],
        out_specs=pl.BlockSpec(memory_space=pltpu.VMEM),
        scratch_shapes=[
            pltpu.VMEM((rows, per_row) + block, BF16),
            pltpu.VMEM((rows,) + block, BF16),
            pltpu.VMEM((n_dom,) + block, BF16),
            pltpu.VMEM((n_dom,) + block, BF16),
            pltpu.VMEM((2, rows) + block, BF16),
            pltpu.VMEM((items + 1,) + block, F32),
            pltpu.VMEM((3 * rows + n_dom, size, 2 * size), BF16),
            pltpu.VMEM((table_rows, 128), jnp.int32),
            pltpu.SMEM((table_rows, 128), jnp.int32),
            dma((rows,)), dma, dma,
            dma((n_dom,)), dma((n_dom,)), dma((2,)), dma((2,)),
        ],
        compiler_params=pltpu.CompilerParams(
            collective_id=0, has_side_effects=True, vmem_limit_bytes=60 * 1024 * 1024
        ),
        cost_estimate=pl.CostEstimate(
            flops=2 * (items + 2 * codes_of(rows, n_dom)) * size**3,
            bytes_accessed=2 * size * size * (items + rows + n_dom + 2),
            transcendentals=0,
        ),
    )(a_cols, send_rows.reshape(-1), a_blocks, p_blocks)


def codes_of(rows, n_dom):
    return 3 * rows + n_dom


def solution(mesh):
    placed = (
        P(("sub", "dom"), None),
        P(("sub", "dom"), None, None, None),
        P(("sub", "dom"), None, None),
        P(("sub", "dom"), None),
    )
    return jax.shard_map(
        functools.partial(per_device, mesh.shape["sub"], mesh.shape["dom"]),
        mesh=mesh,
        in_specs=placed,
        out_specs=P(("sub", "dom"), None, None),
        check_vma=False,
    )
```

```python
import functools

import jax
import jax.numpy as jnp
from jax import lax
from jax.experimental import pallas as pl
from jax.experimental.pallas import tpu as pltpu
from jax.sharding import PartitionSpec as P

MESH = pl.DeviceIdType.MESH
F32 = jnp.float32
BF16 = jnp.bfloat16


def kernel(
    n_sub, n_dom, rows, per_row, size,
    cols, send_rows, a_hbm, p_hbm, out,
    a_buf, p_buf, stage, far, near, part, pairs, table, links,
    a_sem, p_sem, link_sem, far_send, far_recv, near_send, near_recv, root_in,
):
    sub, dom = lax.axis_index("sub"), lax.axis_index("dom")
    items = rows * per_row
    codes = 3 * rows + n_dom

    root = (sub == 0) & (dom == 0)
    has_below, has_above = sub > 0, sub < n_sub - 1
    root_far = (sub == 0) & (dom > 0)
    root_near = (sub == 1) & (dom == 0)
    meets_root = root_far | root_near
    one = jnp.int32(1)

    def count(flag):
        return jnp.where(flag, one, 0)

    barrier = pltpu.get_barrier_semaphore()

    def greet(other):
        pl.semaphore_signal(barrier, inc=1, device_id=other, device_id_type=MESH)

    p_copy = pltpu.make_async_copy(p_hbm, p_buf, p_sem)
    p_copy.start()
    a_copies = [
        pltpu.make_async_copy(a_hbm.at[r], a_buf.at[r], a_sem.at[r]) for r in range(rows)
    ]
    for copy in a_copies:
        copy.start()

    @pl.when(jnp.logical_not(root))
    def _():
        for step in range(1, n_dom):
            peer = lax.rem(dom + step, n_dom)

            @pl.when(jnp.logical_not((sub == 0) & (peer == 0)))
            def _():
                greet({"dom": peer})

        @pl.when(has_above)
        def _():
            greet({"sub": sub + 1})

        @pl.when(has_below & jnp.logical_not(root_near))
        def _():
            greet({"sub": sub - 1})

    p_copy.wait()

    @pl.loop(1, n_dom)
    def _(step):
        row = jnp.clip(send_rows[lax.rem(dom + step, n_dom)], 0, rows - 1)
        stage[step] = p_buf[row]

    def far_copy(step):
        return pltpu.make_async_remote_copy(
            src_ref=stage.at[step], dst_ref=far.at[step],
            send_sem=far_send.at[step], recv_sem=far_recv.at[step],
            device_id={"dom": lax.rem(dom + step, n_dom)}, device_id_type=MESH,
        )

    def near_copy(place):
        return pltpu.make_async_remote_copy(
            src_ref=p_buf, dst_ref=near.at[place],
            send_sem=near_send.at[place], recv_sem=near_recv.at[place],
            device_id={"sub": sub + 1 - 2 * place}, device_id_type=MESH,
        )

    def to_root(step):
        return (sub == 0) & (lax.rem(dom + step, n_dom) == 0)

    def from_root(step):
        return (sub == 0) & (dom == step)

    @pl.when(root)
    def _():
        pl.semaphore_wait(barrier, n_dom)
        for step in range(1, n_dom):
            pl.semaphore_signal(root_in, inc=1, device_id={"dom": dom + step}, device_id_type=MESH)
        pl.semaphore_signal(root_in, inc=1, device_id={"sub": sub + 1}, device_id_type=MESH)

    @pl.when(jnp.logical_not(root))
    def _():
        pl.semaphore_wait(
            barrier, n_dom - 1 + count(has_above) + count(has_below) - count(meets_root)
        )

    @pl.when(root_far)
    def _():
        greet({"dom": 0})

    @pl.when(root_near)
    def _():
        greet({"sub": 0})

    @pl.loop(1, n_dom)
    def _(step):
        @pl.when(jnp.logical_not(to_root(step)))
        def _():
            far_copy(step).start()

    @pl.when(has_above)
    def _():
        near_copy(0).start()

    @pl.when(has_below & jnp.logical_not(root_near))
    def _():
        near_copy(1).start()

    lane = lax.broadcasted_iota(jnp.int32, (1, 128), 1)
    last = jnp.full((1, 128), items, jnp.int32)
    for j in range(items):
        table[pl.ds(j, 1), :] = last
        last = jnp.where(lane == cols[j // per_row, j % per_row], j, last)
    table[pl.ds(items, 1), :] = last
    link_copy = pltpu.make_async_copy(table, links, link_sem)
    link_copy.start()

    for r in range(rows):
        left = p_buf[r].T
        a_copies[r].wait()
        group = next(g for g in (9, 8, 6, 5, 4, 3, 2, 1) if per_row % g == 0)

        @pl.loop(0, per_row // group)
        def _(block):
            base = block * group
            for k in range(group):
                part[r * per_row + base + k] = jnp.dot(
                    left, a_buf[r, base + k], preferred_element_type=F32
                )

    part[items] = jnp.zeros((size, size), F32)
    link_copy.wait()
    for r in range(rows):

        @pl.loop(0, per_row)
        def _(k):
            j = r * per_row + k
            part[j] += part[links[j, cols[r, k]]]

    @pl.loop(0, codes)
    def _(v):
        total = part[links[items, v]]
        high = total.astype(BF16)
        low = (total - high.astype(F32)).astype(BF16)
        pairs[v] = jnp.concatenate([high, low], axis=1)

    def window(first, blocks):
        left = jnp.concatenate([pairs[first + i] for i in range(len(blocks))], axis=1)
        right = jnp.concatenate([b for b in blocks for _ in range(2)], axis=0)
        return jnp.dot(left, right, preferred_element_type=F32).astype(BF16)

    def put(place, value):
        out[0, :, pl.ds(pl.multiple_of(place * size, size), size)] = value

    put(dom, window(rows, [p_buf[r] for r in range(rows)]))

    def take_near(place):
        near_copy(place).wait_recv()
        put(n_dom + place, window(2 * rows * place, [near[place, r] for r in range(rows)]))

    def take_far(step):
        far_copy(step).wait_recv()
        source = lax.rem(dom + n_dom - step, n_dom)
        put(source, window(3 * rows + source, [far[step]]))

    @pl.when(has_below & jnp.logical_not(root_near))
    def _():
        take_near(0)

    @pl.when(has_above)
    def _():
        take_near(1)

    for place, there in ((0, has_below), (1, has_above)):

        @pl.when(jnp.logical_not(there))
        def _():
            put(n_dom + place, jnp.zeros((size, size), BF16))

    @pl.loop(1, n_dom)
    def _(step):
        @pl.when(jnp.logical_not(from_root(step)))
        def _():
            take_far(step)

    @pl.loop(1, n_dom)
    def _(step):
        @pl.when(jnp.logical_not(to_root(step)))
        def _():
            far_copy(step).wait_send()

    @pl.when(has_above)
    def _():
        near_copy(0).wait_send()

    @pl.when(has_below & jnp.logical_not(root_near))
    def _():
        near_copy(1).wait_send()

    @pl.when(root_far)
    def _():
        pl.semaphore_wait(root_in, 1)
        far_copy(n_dom - dom).start()
        take_far(dom)
        far_copy(n_dom - dom).wait_send()

    @pl.when(root_near)
    def _():
        pl.semaphore_wait(root_in, 1)
        near_copy(1).start()
        take_near(0)
        near_copy(1).wait_send()


def per_device(n_sub, n_dom, a_cols, a_blocks, p_blocks, send_rows):
    rows, per_row = a_cols.shape
    size = p_blocks.shape[1]
    items = rows * per_row
    table_rows = (items + 8) // 8 * 8
    block = (size, size)
    dma = pltpu.SemaphoreType.DMA
    operands = (a_cols, send_rows.reshape(-1), a_blocks, p_blocks)
    return pl.pallas_call(
        functools.partial(kernel, n_sub, n_dom, rows, per_row, size),
        out_shape=jax.ShapeDtypeStruct((1, size, (n_dom + 2) * size), BF16),
        in_specs=[
            pl.BlockSpec(memory_space=pltpu.SMEM),
            pl.BlockSpec(memory_space=pltpu.SMEM),
            pl.BlockSpec(memory_space=pltpu.HBM),
            pl.BlockSpec(memory_space=pltpu.HBM),
        ],
        out_specs=pl.BlockSpec(memory_space=pltpu.VMEM),
        scratch_shapes=[
            pltpu.VMEM((rows, per_row) + block, BF16),
            pltpu.VMEM((rows,) + block, BF16),
            pltpu.VMEM((n_dom,) + block, BF16),
            pltpu.VMEM((n_dom,) + block, BF16),
            pltpu.VMEM((2, rows) + block, BF16),
            pltpu.VMEM((items + 1,) + block, F32),
            pltpu.VMEM((3 * rows + n_dom, size, 2 * size), BF16),
            pltpu.VMEM((table_rows, 128), jnp.int32),
            pltpu.SMEM((table_rows, 128), jnp.int32),
            dma((rows,)), dma, dma,
            dma((n_dom,)), dma((n_dom,)), dma((2,)), dma((2,)), pltpu.SemaphoreType.REGULAR,
        ],
        compiler_params=pltpu.CompilerParams(
            collective_id=0, has_side_effects=True, vmem_limit_bytes=48 * 1024 * 1024
        ),
        cost_estimate=pl.CostEstimate(
            flops=2 * (items + 2 * codes_of(rows, n_dom)) * size**3,
            bytes_accessed=2 * size * size * (items + rows + n_dom + 2),
            transcendentals=0,
        ),
    )(*(pltpu.with_memory_space_constraint(x, pltpu.HBM) for x in operands))


def codes_of(rows, n_dom):
    return 3 * rows + n_dom


def solution(mesh):
    placed = (
        P(("sub", "dom"), None),
        P(("sub", "dom"), None, None, None),
        P(("sub", "dom"), None, None),
        P(("sub", "dom"), None),
    )
    return jax.shard_map(
        functools.partial(per_device, mesh.shape["sub"], mesh.shape["dom"]),
        mesh=mesh,
        in_specs=placed,
        out_specs=P(("sub", "dom"), None, None),
        check_vma=False,
    )
```

```python
import functools

import jax
import jax.numpy as jnp
from jax import lax
from jax.experimental import pallas as pl
from jax.experimental.pallas import tpu as pltpu
from jax.sharding import PartitionSpec as P

MESH = pl.DeviceIdType.MESH
F32 = jnp.float32
BF16 = jnp.bfloat16


def far_first(size):
    return sorted(range(size), key=lambda k: (-min(k, size - k), k))


def near_first(long_side, side):
    def order(offset):
        x, y = offset // side, offset % side
        steps = min(x, long_side - x) + min(y, side - y)
        return (2 if x == 0 else int(x > long_side // 2), steps, offset)

    return sorted(range(1, long_side * side), key=order)


def pick(values, i):
    value = jnp.int32(values[-1])
    for k, v in enumerate(values[:-1]):
        value = jnp.where(i == k, jnp.int32(v), value)
    return value


def kernel(
    n_sub, n_dom, rows, per_row, size,
    cols_hbm, send_hbm, a_hbm, p_hbm, out,
    cols, send_rows, a_buf, p_buf, stage, far, near, part, pairs, table, links,
    cols_sem, send_rows_sem, a_sem, p_sem, link_sem, far_send, far_recv, near_send, near_recv, root_in,
):
    sub, dom = lax.axis_index("sub"), lax.axis_index("dom")
    items = rows * per_row
    codes = 3 * rows + n_dom
    side = max(k for k in range(1, n_dom + 1) if n_dom % k == 0 and k * k <= n_dom)
    long_side = n_dom // side

    root = (sub == 0) & (dom == 0)
    has_below, has_above = sub > 0, sub < n_sub - 1
    root_far = (sub == 0) & (dom > 0)
    root_near = (sub == 1) & (dom == 0)
    meets_root = root_far | root_near
    one = jnp.int32(1)

    def count(flag):
        return jnp.where(flag, one, 0)

    barrier = pltpu.get_barrier_semaphore()

    def greet(other):
        pl.semaphore_signal(barrier, inc=1, device_id=other, device_id_type=MESH)

    send_rows_copy = pltpu.make_async_copy(send_hbm, send_rows, send_rows_sem)
    send_rows_copy.start()
    half = size // 2
    p_copies = [
        pltpu.make_async_copy(
            p_hbm.at[r, pl.ds(h * half, half)], p_buf.at[r, pl.ds(h * half, half)],
            p_sem.at[2 * r + h],
        )
        for r in range(rows)
        for h in range(2)
    ]
    for copy in p_copies:
        copy.start()
    cols_copy = pltpu.make_async_copy(cols_hbm, cols, cols_sem)
    cols_copy.start()
    a_copies = [
        pltpu.make_async_copy(a_hbm.at[r], a_buf.at[r], a_sem.at[r]) for r in range(rows)
    ]

    @pl.when(jnp.logical_not(root))
    def _():
        for step in range(1, n_dom):
            peer = lax.rem(dom + step, n_dom)

            @pl.when(jnp.logical_not((sub == 0) & (peer == 0)))
            def _():
                greet({"dom": peer})

        @pl.when(has_above)
        def _():
            greet({"sub": sub + 1})

        @pl.when(has_below & jnp.logical_not(root_near))
        def _():
            greet({"sub": sub - 1})

    def peer_at(offset, sign):
        x = lax.rem(dom // side + long_side + sign * (offset // side), long_side)
        y = lax.rem(dom % side + side + sign * (offset % side), side)
        return x * side + y

    def offset_at(i):
        return pick(far_first(long_side), i // side) * side + pick(far_first(side), i % side)

    def put_on_stage(offset):
        row = jnp.clip(send_rows[peer_at(offset, 1)], 0, rows - 1)
        stage[offset] = p_buf[row]

    def far_copy(offset):
        return pltpu.make_async_remote_copy(
            src_ref=stage.at[offset], dst_ref=far.at[offset],
            send_sem=far_send.at[offset], recv_sem=far_recv.at[offset],
            device_id={"dom": peer_at(offset, 1)}, device_id_type=MESH,
        )

    def near_copy(place):
        return pltpu.make_async_remote_copy(
            src_ref=p_buf, dst_ref=near.at[place],
            send_sem=near_send.at[place], recv_sem=near_recv.at[place],
            device_id={"sub": sub + 1 - 2 * place}, device_id_type=MESH,
        )

    def to_root(offset):
        return (sub == 0) & (peer_at(offset, 1) == 0)

    def from_root(offset):
        return (sub == 0) & (dom == offset)

    @pl.when(root)
    def _():
        pl.semaphore_wait(barrier, n_dom)
        for step in range(1, n_dom):
            pl.semaphore_signal(root_in, inc=1, device_id={"dom": step}, device_id_type=MESH)
        pl.semaphore_signal(root_in, inc=1, device_id={"sub": 1}, device_id_type=MESH)
        send_rows_copy.wait()
        for copy in p_copies:
            copy.wait()
        for offset in near_first(long_side, side):
            put_on_stage(offset)
            far_copy(offset).start()
        near_copy(0).start()
        for copy in a_copies:
            copy.start()

    @pl.when(jnp.logical_not(root))
    def _():
        for copy in a_copies:
            copy.start()
        send_rows_copy.wait()
        for copy in p_copies:
            copy.wait()

        @pl.loop(1, n_dom)
        def _(offset):
            put_on_stage(offset)

        pl.semaphore_wait(
            barrier, n_dom - 1 + count(has_above) + count(has_below) - count(meets_root)
        )

        @pl.when(root_far)
        def _():
            greet({"dom": 0})

        @pl.when(root_near)
        def _():
            greet({"sub": 0})

        @pl.loop(0, n_dom - 1)
        def _(i):
            offset = offset_at(i)

            @pl.when(jnp.logical_not(to_root(offset)))
            def _():
                far_copy(offset).start()

        @pl.when(has_above)
        def _():
            near_copy(0).start()

        @pl.when(has_below & jnp.logical_not(root_near))
        def _():
            near_copy(1).start()

    cols_copy.wait()
    lane = lax.broadcasted_iota(jnp.int32, (1, 128), 1)
    last = jnp.full((1, 128), items, jnp.int32)
    for j in range(items):
        table[pl.ds(j, 1), :] = last
        last = jnp.where(lane == cols[j // per_row, j % per_row], j, last)
    table[pl.ds(items, 1), :] = last
    link_copy = pltpu.make_async_copy(table, links, link_sem)
    link_copy.start()

    for r in range(rows):
        left = p_buf[r].T
        a_copies[r].wait()
        group = next(g for g in (9, 8, 6, 5, 4, 3, 2, 1) if per_row % g == 0)

        @pl.loop(0, per_row // group)
        def _(block):
            base = block * group
            for k in range(group):
                part[r * per_row + base + k] = jnp.dot(
                    left, a_buf[r, base + k], preferred_element_type=F32
                )

    part[items] = jnp.zeros((size, size), F32)
    link_copy.wait()
    for r in range(rows):

        @pl.loop(0, per_row)
        def _(k):
            j = r * per_row + k
            part[j] += part[links[j, cols[r, k]]]

    @pl.loop(0, codes)
    def _(v):
        total = part[links[items, v]]
        high = total.astype(BF16)
        low = (total - high.astype(F32)).astype(BF16)
        pairs[v] = jnp.concatenate([high, low], axis=1)

    def window(first, blocks):
        left = jnp.concatenate([pairs[first + i] for i in range(len(blocks))], axis=1)
        right = jnp.concatenate([b for b in blocks for _ in range(2)], axis=0)
        return jnp.dot(left, right, preferred_element_type=F32).astype(BF16)

    def put(place, value):
        out[0, :, pl.ds(pl.multiple_of(place * size, size), size)] = value

    put(dom, window(rows, [p_buf[r] for r in range(rows)]))

    def take_near(place):
        near_copy(place).wait_recv()
        put(n_dom + place, window(2 * rows * place, [near[place, r] for r in range(rows)]))

    def take_far(offset):
        far_copy(offset).wait_recv()
        source = peer_at(offset, -1)
        put(source, window(3 * rows + source, [far[offset]]))

    @pl.when(has_below & jnp.logical_not(root_near))
    def _():
        take_near(0)

    @pl.when(has_above)
    def _():
        take_near(1)

    for place, there in ((0, has_below), (1, has_above)):

        @pl.when(jnp.logical_not(there))
        def _():
            put(n_dom + place, jnp.zeros((size, size), BF16))

    @pl.loop(0, n_dom - 1)
    def _(i):
        offset = offset_at(i)

        @pl.when(jnp.logical_not(from_root(offset)))
        def _():
            take_far(offset)

    @pl.loop(1, n_dom)
    def _(offset):
        @pl.when(jnp.logical_not(to_root(offset)))
        def _():
            far_copy(offset).wait_send()

    @pl.when(has_above)
    def _():
        near_copy(0).wait_send()

    @pl.when(has_below & jnp.logical_not(root_near))
    def _():
        near_copy(1).wait_send()

    @pl.when(root_far)
    def _():
        pl.semaphore_wait(root_in, 1)
        back = (
            lax.rem(long_side - dom // side, long_side) * side + lax.rem(side - dom % side, side)
        )
        far_copy(back).start()
        take_far(dom)
        far_copy(back).wait_send()

    @pl.when(root_near)
    def _():
        pl.semaphore_wait(root_in, 1)
        near_copy(1).start()
        take_near(0)
        near_copy(1).wait_send()


def per_device(n_sub, n_dom, a_cols, a_blocks, p_blocks, send_rows):
    rows, per_row = a_cols.shape
    size = p_blocks.shape[1]
    items = rows * per_row
    table_rows = (items + 8) // 8 * 8
    block = (size, size)
    dma = pltpu.SemaphoreType.DMA
    operands = (a_cols, send_rows.reshape(-1), a_blocks, p_blocks)
    return pl.pallas_call(
        functools.partial(kernel, n_sub, n_dom, rows, per_row, size),
        out_shape=jax.ShapeDtypeStruct((1, size, (n_dom + 2) * size), BF16),
        in_specs=[pl.BlockSpec(memory_space=pltpu.HBM)] * 4,
        out_specs=pl.BlockSpec(memory_space=pltpu.VMEM),
        scratch_shapes=[
            pltpu.SMEM(operands[0].shape, jnp.int32),
            pltpu.SMEM(operands[1].shape, jnp.int32),
            pltpu.VMEM((rows, per_row) + block, BF16),
            pltpu.VMEM((rows,) + block, BF16),
            pltpu.VMEM((n_dom,) + block, BF16),
            pltpu.VMEM((n_dom,) + block, BF16),
            pltpu.VMEM((2, rows) + block, BF16),
            pltpu.VMEM((items + 1,) + block, F32),
            pltpu.VMEM((3 * rows + n_dom, size, 2 * size), BF16),
            pltpu.VMEM((table_rows, 128), jnp.int32),
            pltpu.SMEM((table_rows, 128), jnp.int32),
            dma, dma, dma((rows,)), dma((2 * rows,)), dma,
            dma((n_dom,)), dma((n_dom,)), dma((2,)), dma((2,)), pltpu.SemaphoreType.REGULAR,
        ],
        compiler_params=pltpu.CompilerParams(
            collective_id=0, has_side_effects=True, vmem_limit_bytes=48 * 1024 * 1024
        ),
        cost_estimate=pl.CostEstimate(
            flops=2 * (items + 2 * codes_of(rows, n_dom)) * size**3,
            bytes_accessed=2 * size * size * (items + rows + n_dom + 2),
            transcendentals=0,
        ),
    )(*(pltpu.with_memory_space_constraint(x, pltpu.HBM) for x in operands))


def codes_of(rows, n_dom):
    return 3 * rows + n_dom


def solution(mesh):
    placed = (
        P(("sub", "dom"), None),
        P(("sub", "dom"), None, None, None),
        P(("sub", "dom"), None, None),
        P(("sub", "dom"), None),
    )
    return jax.shard_map(
        functools.partial(per_device, mesh.shape["sub"], mesh.shape["dom"]),
        mesh=mesh,
        in_specs=placed,
        out_specs=P(("sub", "dom"), None, None),
        check_vma=False,
    )
```

```python
import functools

import jax
import jax.numpy as jnp
from jax import lax
from jax.experimental import pallas as pl
from jax.experimental.pallas import tpu as pltpu
from jax.sharding import PartitionSpec as P

MESH = pl.DeviceIdType.MESH
F32 = jnp.float32
BF16 = jnp.bfloat16


def far_first(size):
    return sorted(range(size), key=lambda k: (-min(k, size - k), k))


def near_first(long_side, side):
    def order(offset):
        x, y = offset // side, offset % side
        steps = min(x, long_side - x) + min(y, side - y)
        return (2 if x == 0 else int(x > long_side // 2), steps, offset)

    return sorted(range(1, long_side * side), key=order)


def pick(values, i):
    value = jnp.int32(values[-1])
    for k, v in enumerate(values[:-1]):
        value = jnp.where(i == k, jnp.int32(v), value)
    return value


def kernel(
    n_sub, n_dom, rows, per_row, size,
    cols_hbm, send_hbm, a_hbm, p_hbm, out,
    cols, send_rows, a_buf, p_buf, stage, far, near, part, pairs, table, links,
    cols_sem, send_rows_sem, a_sem, p_sem, link_sem, far_send, far_recv, near_send, near_recv, root_in,
):
    sub, dom = lax.axis_index("sub"), lax.axis_index("dom")
    items = rows * per_row
    codes = 3 * rows + n_dom
    side = max(k for k in range(1, n_dom + 1) if n_dom % k == 0 and k * k <= n_dom)
    long_side = n_dom // side

    root = (sub == 0) & (dom == 0)
    has_below, has_above = sub > 0, sub < n_sub - 1
    root_far = (sub == 0) & (dom > 0)
    root_near = (sub == 1) & (dom == 0)
    meets_root = root_far | root_near
    one = jnp.int32(1)

    def count(flag):
        return jnp.where(flag, one, 0)

    barrier = pltpu.get_barrier_semaphore()

    def greet(other):
        pl.semaphore_signal(barrier, inc=1, device_id=other, device_id_type=MESH)

    send_rows_copy = pltpu.make_async_copy(send_hbm, send_rows, send_rows_sem)
    send_rows_copy.start()
    half = size // 2
    p_copies = [
        pltpu.make_async_copy(
            p_hbm.at[r, pl.ds(h * half, half)], p_buf.at[r, pl.ds(h * half, half)],
            p_sem.at[2 * r + h],
        )
        for r in range(rows)
        for h in range(2)
    ]
    for copy in p_copies:
        copy.start()
    cols_copy = pltpu.make_async_copy(cols_hbm, cols, cols_sem)
    cols_copy.start()
    a_copies = [
        pltpu.make_async_copy(a_hbm.at[r], a_buf.at[r], a_sem.at[r]) for r in range(rows)
    ]

    @pl.when(jnp.logical_not(root))
    def _():
        for step in range(1, n_dom):
            peer = lax.rem(dom + step, n_dom)

            @pl.when(jnp.logical_not((sub == 0) & (peer == 0)))
            def _():
                greet({"dom": peer})

        @pl.when(has_above)
        def _():
            greet({"sub": sub + 1})

        @pl.when(has_below & jnp.logical_not(root_near))
        def _():
            greet({"sub": sub - 1})

    def peer_at(offset, sign):
        x = lax.rem(dom // side + long_side + sign * (offset // side), long_side)
        y = lax.rem(dom % side + side + sign * (offset % side), side)
        return x * side + y

    def offset_at(i):
        return pick(far_first(long_side), i // side) * side + pick(far_first(side), i % side)

    def put_on_stage(offset):
        row = jnp.clip(send_rows[peer_at(offset, 1)], 0, rows - 1)
        stage[offset] = p_buf[row]

    def far_copy(offset, sender=0):
        return pltpu.make_async_remote_copy(
            src_ref=stage.at[offset], dst_ref=far.at[offset],
            send_sem=far_send.at[sender], recv_sem=far_recv.at[offset],
            device_id={"dom": peer_at(offset, 1)}, device_id_type=MESH,
        )

    def near_copy(place):
        return pltpu.make_async_remote_copy(
            src_ref=p_buf, dst_ref=near.at[place],
            send_sem=near_send.at[place], recv_sem=near_recv.at[place],
            device_id={"sub": sub + 1 - 2 * place}, device_id_type=MESH,
        )

    def to_root(offset):
        return (sub == 0) & (peer_at(offset, 1) == 0)

    def from_root(offset):
        return (sub == 0) & (dom == offset)

    @pl.when(root)
    def _():
        pl.semaphore_wait(barrier, n_dom)
        for step in range(1, n_dom):
            pl.semaphore_signal(root_in, inc=1, device_id={"dom": step}, device_id_type=MESH)
        pl.semaphore_signal(root_in, inc=1, device_id={"sub": 1}, device_id_type=MESH)
        send_rows_copy.wait()
        for copy in p_copies:
            copy.wait()
        for offset in near_first(long_side, side):
            put_on_stage(offset)
            far_copy(offset).start()
        near_copy(0).start()
        for copy in a_copies:
            copy.start()

    @pl.when(jnp.logical_not(root))
    def _():
        for copy in a_copies:
            copy.start()
        send_rows_copy.wait()
        for copy in p_copies:
            copy.wait()

        @pl.loop(1, n_dom)
        def _(offset):
            put_on_stage(offset)

        pl.semaphore_wait(
            barrier, n_dom - 1 + count(has_above) + count(has_below) - count(meets_root)
        )

        @pl.when(root_far)
        def _():
            greet({"dom": 0})

        @pl.when(root_near)
        def _():
            greet({"sub": 0})

        @pl.loop(0, n_dom - 1)
        def _(i):
            offset = offset_at(i)

            @pl.when(jnp.logical_not(to_root(offset)))
            def _():
                far_copy(offset).start()

        @pl.when(has_above)
        def _():
            near_copy(0).start()

        @pl.when(has_below & jnp.logical_not(root_near))
        def _():
            near_copy(1).start()

    cols_copy.wait()
    lane = lax.broadcasted_iota(jnp.int32, (1, 128), 1)
    last = jnp.full((1, 128), items, jnp.int32)
    for j in range(items):
        table[pl.ds(j, 1), :] = last
        last = jnp.where(lane == cols[j // per_row, j % per_row], j, last)
    table[pl.ds(items, 1), :] = last
    link_copy = pltpu.make_async_copy(table, links, link_sem)
    link_copy.start()

    for r in range(rows):
        left = p_buf[r].T
        a_copies[r].wait()
        group = next(g for g in (9, 8, 6, 5, 4, 3, 2, 1) if per_row % g == 0)

        @pl.loop(0, per_row // group)
        def _(block):
            base = block * group
            for k in range(group):
                part[r * per_row + base + k] = jnp.dot(
                    left, a_buf[r, base + k], preferred_element_type=F32
                )

    part[items] = jnp.zeros((size, size), F32)
    link_copy.wait()
    for r in range(rows):

        @pl.loop(0, per_row)
        def _(k):
            j = r * per_row + k
            part[j] += part[links[j, cols[r, k]]]

    @pl.loop(0, codes)
    def _(v):
        total = part[links[items, v]]
        high = total.astype(BF16)
        low = (total - high.astype(F32)).astype(BF16)
        pairs[v] = jnp.concatenate([high, low], axis=1)

    def window(first, blocks):
        left = jnp.concatenate([pairs[first + i] for i in range(len(blocks))], axis=1)
        right = jnp.concatenate([b for b in blocks for _ in range(2)], axis=0)
        return jnp.dot(left, right, preferred_element_type=F32).astype(BF16)

    def put(place, value):
        out[0, :, pl.ds(pl.multiple_of(place * size, size), size)] = value

    put(dom, window(rows, [p_buf[r] for r in range(rows)]))

    def take_near(place):
        near_copy(place).wait_recv()
        put(n_dom + place, window(2 * rows * place, [near[place, r] for r in range(rows)]))

    def take_far(offset):
        far_copy(offset).wait_recv()
        source = peer_at(offset, -1)
        put(source, window(3 * rows + source, [far[offset]]))

    @pl.when(has_below & jnp.logical_not(root_near))
    def _():
        take_near(0)

    @pl.when(has_above)
    def _():
        take_near(1)

    for place, there in ((0, has_below), (1, has_above)):

        @pl.when(jnp.logical_not(there))
        def _():
            put(n_dom + place, jnp.zeros((size, size), BF16))

    def wait_far_sends(number):
        pltpu.make_async_remote_copy(
            src_ref=stage.at[pl.ds(1, number)], dst_ref=far.at[pl.ds(1, number)],
            send_sem=far_send.at[0], recv_sem=far_recv.at[0],
            device_id={"dom": peer_at(1, 1)}, device_id_type=MESH,
        ).wait_send()

    @pl.when(root_far)
    def _():
        wait_far_sends(n_dom - 2)

    @pl.when(jnp.logical_not(root_far))
    def _():
        wait_far_sends(n_dom - 1)

    @pl.when(has_above)
    def _():
        near_copy(0).wait_send()

    @pl.when(has_below & jnp.logical_not(root_near))
    def _():
        near_copy(1).wait_send()

    back = lax.rem(long_side - dom // side, long_side) * side + lax.rem(side - dom % side, side)

    @pl.loop(0, n_dom)
    def _(i):
        last_turn = i == n_dom - 1
        offset = jnp.where(last_turn, dom, offset_at(i))

        @pl.when(last_turn & root_far)
        def _():
            pl.semaphore_wait(root_in, 1)
            far_copy(back, 1).start()

        @pl.when(jnp.where(last_turn, root_far, jnp.logical_not(from_root(offset))))
        def _():
            take_far(offset)

    @pl.when(root_far)
    def _():
        far_copy(back, 1).wait_send()

    @pl.when(root_near)
    def _():
        pl.semaphore_wait(root_in, 1)
        near_copy(1).start()
        take_near(0)
        near_copy(1).wait_send()


def per_device(n_sub, n_dom, a_cols, a_blocks, p_blocks, send_rows):
    rows, per_row = a_cols.shape
    size = p_blocks.shape[1]
    items = rows * per_row
    table_rows = (items + 8) // 8 * 8
    block = (size, size)
    dma = pltpu.SemaphoreType.DMA
    operands = (a_cols, send_rows.reshape(-1), a_blocks, p_blocks)
    return pl.pallas_call(
        functools.partial(kernel, n_sub, n_dom, rows, per_row, size),
        out_shape=jax.ShapeDtypeStruct((1, size, (n_dom + 2) * size), BF16),
        in_specs=[pl.BlockSpec(memory_space=pltpu.HBM)] * 4,
        out_specs=pl.BlockSpec(memory_space=pltpu.VMEM),
        scratch_shapes=[
            pltpu.SMEM(operands[0].shape, jnp.int32),
            pltpu.SMEM(operands[1].shape, jnp.int32),
            pltpu.VMEM((rows, per_row) + block, BF16),
            pltpu.VMEM((rows,) + block, BF16),
            pltpu.VMEM((n_dom,) + block, BF16),
            pltpu.VMEM((n_dom,) + block, BF16),
            pltpu.VMEM((2, rows) + block, BF16),
            pltpu.VMEM((items + 1,) + block, F32),
            pltpu.VMEM((3 * rows + n_dom, size, 2 * size), BF16),
            pltpu.VMEM((table_rows, 128), jnp.int32),
            pltpu.SMEM((table_rows, 128), jnp.int32),
            dma, dma, dma((rows,)), dma((2 * rows,)), dma,
            dma((2,)), dma((n_dom,)), dma((2,)), dma((2,)), pltpu.SemaphoreType.REGULAR,
        ],
        compiler_params=pltpu.CompilerParams(
            collective_id=0, has_side_effects=True, vmem_limit_bytes=48 * 1024 * 1024
        ),
        cost_estimate=pl.CostEstimate(
            flops=2 * (items + 2 * codes_of(rows, n_dom)) * size**3,
            bytes_accessed=2 * size * size * (items + rows + n_dom + 2),
            transcendentals=0,
        ),
    )(*(pltpu.with_memory_space_constraint(x, pltpu.HBM) for x in operands))


def codes_of(rows, n_dom):
    return 3 * rows + n_dom


def solution(mesh):
    placed = (
        P(("sub", "dom"), None),
        P(("sub", "dom"), None, None, None),
        P(("sub", "dom"), None, None),
        P(("sub", "dom"), None),
    )
    return jax.shard_map(
        functools.partial(per_device, mesh.shape["sub"], mesh.shape["dom"]),
        mesh=mesh,
        in_specs=placed,
        out_specs=P(("sub", "dom"), None, None),
        check_vma=False,
    )
```

```python
import functools

import jax
import jax.numpy as jnp
from jax import lax
from jax.experimental import pallas as pl
from jax.experimental.pallas import tpu as pltpu
from jax.sharding import PartitionSpec as P

MESH = pl.DeviceIdType.MESH
F32 = jnp.float32
BF16 = jnp.bfloat16


def far_first(size):
    return sorted(range(size), key=lambda k: (-min(k, size - k), k))


def root_order(long_side, side):
    def order(offset):
        x, y = offset // side, offset % side
        return (2 if x == 0 else int(x > long_side // 2), y, x)

    return sorted(range(1, long_side * side), key=order)


def long_side_of(n_dom):
    return min(k for k in range(1, n_dom + 1) if n_dom % k == 0 and k * k >= n_dom)


def pick(values, i):
    value = jnp.int32(values[-1])
    for k, v in enumerate(values[:-1]):
        value = jnp.where(i == k, jnp.int32(v), value)
    return value


def kernel(
    n_sub, n_dom, rows, per_row, size,
    cols_hbm, send_hbm, a_hbm, p_hbm, out,
    cols, send_rows, a_buf, p_buf, stage, far, near, part, pairs, table, links,
    cols_sem, send_rows_sem, a_sem, p_sem, link_sem, far_send, far_recv, near_send, near_recv, root_in,
):
    sub, dom = lax.axis_index("sub"), lax.axis_index("dom")
    items = rows * per_row
    codes = 3 * rows + n_dom
    long_side = long_side_of(n_dom)
    side = n_dom // long_side

    root = (sub == 0) & (dom == 0)
    has_below, has_above = sub > 0, sub < n_sub - 1
    root_far = (sub == 0) & (dom > 0)
    root_near = (sub == 1) & (dom == 0)
    meets_root = root_far | root_near
    one = jnp.int32(1)

    def count(flag):
        return jnp.where(flag, one, 0)

    barrier = pltpu.get_barrier_semaphore()

    def greet(other):
        pl.semaphore_signal(barrier, inc=1, device_id=other, device_id_type=MESH)

    send_rows_copy = pltpu.make_async_copy(send_hbm, send_rows, send_rows_sem)
    send_rows_copy.start()
    half = size // 2
    p_copies = [
        pltpu.make_async_copy(
            p_hbm.at[r, pl.ds(h * half, half)], p_buf.at[r, pl.ds(h * half, half)],
            p_sem,
        )
        for r in range(rows)
        for h in range(2)
    ]
    p_whole = pltpu.make_async_copy(p_hbm, p_buf, p_sem)
    for copy in p_copies:
        copy.start()
    cols_copy = pltpu.make_async_copy(cols_hbm, cols, cols_sem)
    cols_copy.start()
    a_copies = [
        pltpu.make_async_copy(a_hbm.at[r], a_buf.at[r], a_sem) for r in range(rows)
    ]

    @pl.when(jnp.logical_not(root))
    def _():
        for step in range(1, n_dom):
            peer = lax.rem(dom + step, n_dom)

            @pl.when(jnp.logical_not((sub == 0) & (peer == 0)))
            def _():
                greet({"dom": peer})

        @pl.when(has_above)
        def _():
            greet({"sub": sub + 1})

        @pl.when(has_below & jnp.logical_not(root_near))
        def _():
            greet({"sub": sub - 1})

    def peer_at(offset, sign):
        x = lax.rem(dom // side + long_side + sign * (offset // side), long_side)
        y = lax.rem(dom % side + side + sign * (offset % side), side)
        return x * side + y

    def offset_at(i):
        return pick(far_first(long_side), i // side) * side + pick(far_first(side), i % side)

    def put_on_stage(offset):
        row = jnp.clip(send_rows[peer_at(offset, 1)], 0, rows - 1)
        stage[offset] = p_buf[row]

    def arrival(offset):
        return jnp.where(root, long_side, offset // side)

    def wait_arrivals(group, number):
        pltpu.make_async_remote_copy(
            src_ref=stage.at[pl.ds(0, number)], dst_ref=far.at[pl.ds(0, number)],
            send_sem=far_send.at[0], recv_sem=far_recv.at[group],
            device_id={"dom": peer_at(1, 1)}, device_id_type=MESH,
        ).wait_recv()

    def far_copy(offset, sender=0):
        return pltpu.make_async_remote_copy(
            src_ref=stage.at[offset], dst_ref=far.at[offset],
            send_sem=far_send.at[sender], recv_sem=far_recv.at[arrival(offset)],
            device_id={"dom": peer_at(offset, 1)}, device_id_type=MESH,
        )

    def near_copy(place):
        return pltpu.make_async_remote_copy(
            src_ref=p_buf, dst_ref=near.at[place],
            send_sem=near_send.at[place], recv_sem=near_recv.at[place],
            device_id={"sub": sub + 1 - 2 * place}, device_id_type=MESH,
        )

    def to_root(offset):
        return (sub == 0) & (peer_at(offset, 1) == 0)

    def from_root(offset):
        return (sub == 0) & (dom == offset)

    @pl.when(root)
    def _():
        pl.semaphore_wait(barrier, n_dom)
        for step in range(1, n_dom):
            pl.semaphore_signal(root_in, inc=1, device_id={"dom": step}, device_id_type=MESH)
        pl.semaphore_signal(root_in, inc=1, device_id={"sub": 1}, device_id_type=MESH)
        send_rows_copy.wait()
        p_whole.wait()
        for offset in root_order(long_side, side):
            put_on_stage(offset)
            far_copy(offset).start()
        near_copy(0).start()
        for copy in a_copies:
            copy.start()

    @pl.when(jnp.logical_not(root))
    def _():
        for copy in a_copies:
            copy.start()
        send_rows_copy.wait()
        p_whole.wait()

        @pl.loop(1, n_dom)
        def _(offset):
            put_on_stage(offset)

        pl.semaphore_wait(
            barrier, n_dom - 1 + count(has_above) + count(has_below) - count(meets_root)
        )

        @pl.when(root_far)
        def _():
            greet({"dom": 0})

        @pl.when(root_near)
        def _():
            greet({"sub": 0})

        @pl.loop(0, n_dom - 1)
        def _(i):
            offset = offset_at(i)

            @pl.when(jnp.logical_not(to_root(offset)))
            def _():
                far_copy(offset).start()

        @pl.when(has_above)
        def _():
            near_copy(0).start()

        @pl.when(has_below & jnp.logical_not(root_near))
        def _():
            near_copy(1).start()

    cols_copy.wait()
    lane = lax.broadcasted_iota(jnp.int32, (1, 128), 1)
    last = jnp.full((1, 128), items, jnp.int32)
    for j in range(items):
        table[pl.ds(j, 1), :] = last
        last = jnp.where(lane == cols[j // per_row, j % per_row], j, last)
    table[pl.ds(items, 1), :] = last
    link_copy = pltpu.make_async_copy(table, links, link_sem)
    link_copy.start()

    pltpu.make_async_copy(a_hbm, a_buf, a_sem).wait()

    for r in range(rows):
        left = p_buf[r].T
        group = next(g for g in (9, 8, 6, 5, 4, 3, 2, 1) if per_row % g == 0)

        @pl.loop(0, per_row // group)
        def _(block):
            base = block * group
            for k in range(group):
                part[r * per_row + base + k] = jnp.dot(
                    left, a_buf[r, base + k], preferred_element_type=F32
                )

    part[items] = jnp.zeros((size, size), F32)
    link_copy.wait()
    for r in range(rows):

        @pl.loop(0, per_row)
        def _(k):
            j = r * per_row + k
            part[j] += part[links[j, cols[r, k]]]

    @pl.loop(0, codes)
    def _(v):
        total = part[links[items, v]]
        high = total.astype(BF16)
        low = (total - high.astype(F32)).astype(BF16)
        pairs[v] = jnp.concatenate([high, low], axis=1)

    def window(first, blocks):
        left = jnp.concatenate([pairs[first + i] for i in range(len(blocks))], axis=1)
        right = jnp.concatenate([b for b in blocks for _ in range(2)], axis=0)
        return jnp.dot(left, right, preferred_element_type=F32).astype(BF16)

    def put(place, value):
        out[0, :, pl.ds(pl.multiple_of(place * size, size), size)] = value

    put(dom, window(rows, [p_buf[r] for r in range(rows)]))

    def take_near(place):
        near_copy(place).wait_recv()
        put(n_dom + place, window(2 * rows * place, [near[place, r] for r in range(rows)]))

    def take_far(offset):
        source = peer_at(offset, -1)
        put(source, window(3 * rows + source, [far[offset]]))

    @pl.when(has_below & jnp.logical_not(root_near))
    def _():
        take_near(0)

    @pl.when(has_above)
    def _():
        take_near(1)

    for place, there in ((0, has_below), (1, has_above)):

        @pl.when(jnp.logical_not(there))
        def _():
            put(n_dom + place, jnp.zeros((size, size), BF16))

    def wait_far_sends(number):
        pltpu.make_async_remote_copy(
            src_ref=stage.at[pl.ds(1, number)], dst_ref=far.at[pl.ds(1, number)],
            send_sem=far_send.at[0], recv_sem=far_recv.at[0],
            device_id={"dom": peer_at(1, 1)}, device_id_type=MESH,
        ).wait_send()

    @pl.when(root_far)
    def _():
        wait_far_sends(n_dom - 2)

    @pl.when(jnp.logical_not(root_far))
    def _():
        wait_far_sends(n_dom - 1)

    @pl.when(has_above)
    def _():
        near_copy(0).wait_send()

    @pl.when(has_below & jnp.logical_not(root_near))
    def _():
        near_copy(1).wait_send()

    back = lax.rem(long_side - dom // side, long_side) * side + lax.rem(side - dom % side, side)

    @pl.loop(0, n_dom)
    def _(i):
        last_turn = i == n_dom - 1
        offset = jnp.where(last_turn, dom, offset_at(i))

        @pl.when(last_turn & root_far)
        def _():
            pl.semaphore_wait(root_in, 1)
            far_copy(back, 1).start()
            wait_arrivals(long_side, 1)

        group = offset_at(i) // side
        number = side - count(group == 0) - count(root_far & (dom // side == group))
        for some in range(max(1, side - 2), side + 1):

            @pl.when((i % side == 0) & (number == some))
            def _():
                wait_arrivals(group, some)

        @pl.when(jnp.where(last_turn, root_far, jnp.logical_not(from_root(offset))))
        def _():
            take_far(offset)

    @pl.when(root_far)
    def _():
        far_copy(back, 1).wait_send()

    @pl.when(root_near)
    def _():
        pl.semaphore_wait(root_in, 1)
        near_copy(1).start()
        take_near(0)
        near_copy(1).wait_send()


def per_device(n_sub, n_dom, a_cols, a_blocks, p_blocks, send_rows):
    rows, per_row = a_cols.shape
    size = p_blocks.shape[1]
    items = rows * per_row
    table_rows = (items + 8) // 8 * 8
    block = (size, size)
    dma = pltpu.SemaphoreType.DMA
    operands = (a_cols, send_rows.reshape(-1), a_blocks, p_blocks)
    return pl.pallas_call(
        functools.partial(kernel, n_sub, n_dom, rows, per_row, size),
        out_shape=jax.ShapeDtypeStruct((1, size, (n_dom + 2) * size), BF16),
        in_specs=[pl.BlockSpec(memory_space=pltpu.HBM)] * 4,
        out_specs=pl.BlockSpec(memory_space=pltpu.VMEM),
        scratch_shapes=[
            pltpu.SMEM(operands[0].shape, jnp.int32),
            pltpu.SMEM(operands[1].shape, jnp.int32),
            pltpu.VMEM((rows, per_row) + block, BF16),
            pltpu.VMEM((rows,) + block, BF16),
            pltpu.VMEM((n_dom,) + block, BF16),
            pltpu.VMEM((n_dom,) + block, BF16),
            pltpu.VMEM((2, rows) + block, BF16),
            pltpu.VMEM((items + 1,) + block, F32),
            pltpu.VMEM((3 * rows + n_dom, size, 2 * size), BF16),
            pltpu.VMEM((table_rows, 128), jnp.int32),
            pltpu.SMEM((table_rows, 128), jnp.int32),
            dma, dma, dma, dma, dma,
            dma((2,)), dma((long_side_of(n_dom) + 1,)), dma((2,)), dma((2,)), pltpu.SemaphoreType.REGULAR,
        ],
        compiler_params=pltpu.CompilerParams(
            collective_id=0, has_side_effects=True, vmem_limit_bytes=48 * 1024 * 1024
        ),
        cost_estimate=pl.CostEstimate(
            flops=2 * (items + 2 * codes_of(rows, n_dom)) * size**3,
            bytes_accessed=2 * size * size * (items + rows + n_dom + 2),
            transcendentals=0,
        ),
    )(*(pltpu.with_memory_space_constraint(x, pltpu.HBM) for x in operands))


def codes_of(rows, n_dom):
    return 3 * rows + n_dom


def solution(mesh):
    placed = (
        P(("sub", "dom"), None),
        P(("sub", "dom"), None, None, None),
        P(("sub", "dom"), None, None),
        P(("sub", "dom"), None),
    )
    return jax.shard_map(
        functools.partial(per_device, mesh.shape["sub"], mesh.shape["dom"]),
        mesh=mesh,
        in_specs=placed,
        out_specs=P(("sub", "dom"), None, None),
        check_vma=False,
    )
```

```python
import functools

import jax
import jax.numpy as jnp
from jax import lax
from jax.experimental import pallas as pl
from jax.experimental.pallas import tpu as pltpu
from jax.sharding import PartitionSpec as P

MESH = pl.DeviceIdType.MESH
F32 = jnp.float32
BF16 = jnp.bfloat16


def far_first(size):
    return sorted(range(size), key=lambda k: (-min(k, size - k), k))


def root_order(long_side, side):
    def order(offset):
        x, y = offset // side, offset % side
        return (2 if x == 0 else int(x > long_side // 2), y, x)

    return sorted(range(1, long_side * side), key=order)


def long_side_of(n_dom):
    return min(k for k in range(1, n_dom + 1) if n_dom % k == 0 and k * k >= n_dom)


def pick(values, i):
    value = jnp.int32(values[-1])
    for k, v in enumerate(values[:-1]):
        value = jnp.where(i == k, jnp.int32(v), value)
    return value


def kernel(
    n_sub, n_dom, rows, per_row, size,
    cols_hbm, send_hbm, a_hbm, p_hbm, out,
    cols, send_rows, a_buf, p_buf, stage, far, near, part, pairs, table, links,
    cols_sem, send_rows_sem, a_sem, p_sem, link_sem, far_send, far_recv, near_send, near_recv, root_in,
):
    sub, dom = lax.axis_index("sub"), lax.axis_index("dom")
    items = rows * per_row
    codes = 3 * rows + n_dom
    long_side = long_side_of(n_dom)
    side = n_dom // long_side

    root = (sub == 0) & (dom == 0)
    has_below, has_above = sub > 0, sub < n_sub - 1
    root_far = (sub == 0) & (dom > 0)
    root_near = (sub == 1) & (dom == 0)
    meets_root = root_far | root_near
    one = jnp.int32(1)

    def count(flag):
        return jnp.where(flag, one, 0)

    barrier = pltpu.get_barrier_semaphore()

    def greet(other):
        pl.semaphore_signal(barrier, inc=1, device_id=other, device_id_type=MESH)

    send_rows_copy = pltpu.make_async_copy(send_hbm, send_rows, send_rows_sem)
    send_rows_copy.start()
    piece = size // 4
    p_copies = [
        pltpu.make_async_copy(
            p_hbm.at[r, pl.ds(h * piece, piece)], p_buf.at[r, pl.ds(h * piece, piece)],
            p_sem,
        )
        for r in range(rows)
        for h in range(size // piece)
    ]
    p_whole = pltpu.make_async_copy(p_hbm, p_buf, p_sem)
    for copy in p_copies:
        copy.start()
    cols_copy = pltpu.make_async_copy(cols_hbm, cols, cols_sem)
    cols_copy.start()
    a_copies = [
        pltpu.make_async_copy(a_hbm.at[r], a_buf.at[r], a_sem) for r in range(rows)
    ]

    @pl.when(jnp.logical_not(root))
    def _():
        for step in range(1, n_dom):
            peer = lax.rem(dom + step, n_dom)

            @pl.when(jnp.logical_not((sub == 0) & (peer == 0)))
            def _():
                greet({"dom": peer})

        @pl.when(has_above)
        def _():
            greet({"sub": sub + 1})

        @pl.when(has_below & jnp.logical_not(root_near))
        def _():
            greet({"sub": sub - 1})

    def peer_at(offset, sign):
        x = lax.rem(dom // side + long_side + sign * (offset // side), long_side)
        y = lax.rem(dom % side + side + sign * (offset % side), side)
        return x * side + y

    def offset_at(i):
        return pick(far_first(long_side), i // side) * side + pick(far_first(side), i % side)

    def put_on_stage(offset):
        row = jnp.clip(send_rows[peer_at(offset, 1)], 0, rows - 1)
        stage[offset] = p_buf[row]

    def arrival(offset):
        return jnp.where(root, long_side, offset // side)

    def wait_arrivals(group, number):
        pltpu.make_async_remote_copy(
            src_ref=stage.at[pl.ds(0, number)], dst_ref=far.at[pl.ds(0, number)],
            send_sem=far_send.at[0], recv_sem=far_recv.at[group],
            device_id={"dom": peer_at(1, 1)}, device_id_type=MESH,
        ).wait_recv()

    def far_copy(offset, sender=0):
        return pltpu.make_async_remote_copy(
            src_ref=stage.at[offset], dst_ref=far.at[offset],
            send_sem=far_send.at[sender], recv_sem=far_recv.at[arrival(offset)],
            device_id={"dom": peer_at(offset, 1)}, device_id_type=MESH,
        )

    def near_copy(place):
        return pltpu.make_async_remote_copy(
            src_ref=p_buf, dst_ref=near.at[place],
            send_sem=near_send.at[place], recv_sem=near_recv.at[place],
            device_id={"sub": sub + 1 - 2 * place}, device_id_type=MESH,
        )

    def to_root(offset):
        return (sub == 0) & (peer_at(offset, 1) == 0)

    def from_root(offset):
        return (sub == 0) & (dom == offset)

    @pl.when(root)
    def _():
        pl.semaphore_wait(barrier, n_dom)
        for step in range(1, n_dom):
            pl.semaphore_signal(root_in, inc=1, device_id={"dom": step}, device_id_type=MESH)
        pl.semaphore_signal(root_in, inc=1, device_id={"sub": 1}, device_id_type=MESH)
        send_rows_copy.wait()
        p_whole.wait()
        for offset in root_order(long_side, side):
            put_on_stage(offset)
            far_copy(offset).start()
        near_copy(0).start()
        for copy in a_copies:
            copy.start()

    @pl.when(jnp.logical_not(root))
    def _():
        for copy in a_copies:
            copy.start()
        send_rows_copy.wait()
        p_whole.wait()

        @pl.loop(1, n_dom)
        def _(offset):
            put_on_stage(offset)

        pl.semaphore_wait(
            barrier, n_dom - 1 + count(has_above) + count(has_below) - count(meets_root)
        )

        @pl.when(root_far)
        def _():
            greet({"dom": 0})

        @pl.when(root_near)
        def _():
            greet({"sub": 0})

        @pl.loop(0, n_dom - 1)
        def _(i):
            offset = offset_at(i)

            @pl.when(jnp.logical_not(to_root(offset)))
            def _():
                far_copy(offset).start()

        @pl.when(has_above)
        def _():
            near_copy(0).start()

        @pl.when(has_below & jnp.logical_not(root_near))
        def _():
            near_copy(1).start()

    cols_copy.wait()
    lane = lax.broadcasted_iota(jnp.int32, (1, 128), 1)
    last = jnp.full((1, 128), items, jnp.int32)
    for j in range(items):
        table[pl.ds(j, 1), :] = last
        last = jnp.where(lane == cols[j // per_row, j % per_row], j, last)
    table[pl.ds(items, 1), :] = last
    link_copy = pltpu.make_async_copy(table, links, link_sem)
    link_copy.start()

    pltpu.make_async_copy(a_hbm, a_buf, a_sem).wait()

    for r in range(rows):
        left = p_buf[r].T
        group = next(g for g in (9, 8, 6, 5, 4, 3, 2, 1) if per_row % g == 0)

        @pl.loop(0, per_row // group)
        def _(block):
            base = block * group
            for k in range(group):
                part[r * per_row + base + k] = jnp.dot(
                    left, a_buf[r, base + k], preferred_element_type=F32
                )

    part[items] = jnp.zeros((size, size), F32)
    link_copy.wait()
    for r in range(rows):

        @pl.loop(0, per_row)
        def _(k):
            j = r * per_row + k
            part[j] += part[links[j, cols[r, k]]]

    @pl.loop(0, codes)
    def _(v):
        total = part[links[items, v]]
        high = total.astype(BF16)
        low = (total - high.astype(F32)).astype(BF16)
        pairs[v] = jnp.concatenate([high, low], axis=1)

    def window(first, blocks):
        left = jnp.concatenate([pairs[first + i] for i in range(len(blocks))], axis=1)
        right = jnp.concatenate([b for b in blocks for _ in range(2)], axis=0)
        return jnp.dot(left, right, preferred_element_type=F32).astype(BF16)

    def put(place, value):
        out[0, :, pl.ds(pl.multiple_of(place * size, size), size)] = value

    put(dom, window(rows, [p_buf[r] for r in range(rows)]))

    def take_near(place):
        near_copy(place).wait_recv()
        put(n_dom + place, window(2 * rows * place, [near[place, r] for r in range(rows)]))

    def take_far(offset):
        source = peer_at(offset, -1)
        put(source, window(3 * rows + source, [far[offset]]))

    @pl.when(has_below & jnp.logical_not(root_near))
    def _():
        take_near(0)

    @pl.when(has_above)
    def _():
        take_near(1)

    for place, there in ((0, has_below), (1, has_above)):

        @pl.when(jnp.logical_not(there))
        def _():
            put(n_dom + place, jnp.zeros((size, size), BF16))

    def wait_far_sends(number):
        pltpu.make_async_remote_copy(
            src_ref=stage.at[pl.ds(1, number)], dst_ref=far.at[pl.ds(1, number)],
            send_sem=far_send.at[0], recv_sem=far_recv.at[0],
            device_id={"dom": peer_at(1, 1)}, device_id_type=MESH,
        ).wait_send()

    @pl.when(root_far)
    def _():
        wait_far_sends(n_dom - 2)

    @pl.when(jnp.logical_not(root_far))
    def _():
        wait_far_sends(n_dom - 1)

    @pl.when(has_above)
    def _():
        near_copy(0).wait_send()

    @pl.when(has_below & jnp.logical_not(root_near))
    def _():
        near_copy(1).wait_send()

    back = lax.rem(long_side - dom // side, long_side) * side + lax.rem(side - dom % side, side)

    @pl.loop(0, n_dom)
    def _(i):
        last_turn = i == n_dom - 1
        offset = jnp.where(last_turn, dom, offset_at(i))

        @pl.when(last_turn & root_far)
        def _():
            pl.semaphore_wait(root_in, 1)
            far_copy(back, 1).start()
            wait_arrivals(long_side, 1)

        group = offset_at(i) // side
        number = side - count(group == 0) - count(root_far & (dom // side == group))
        for some in range(max(1, side - 2), side + 1):

            @pl.when((i % side == 0) & (number == some))
            def _():
                wait_arrivals(group, some)

        @pl.when(jnp.where(last_turn, root_far, jnp.logical_not(from_root(offset))))
        def _():
            take_far(offset)

    @pl.when(root_far)
    def _():
        far_copy(back, 1).wait_send()

    @pl.when(root_near)
    def _():
        pl.semaphore_wait(root_in, 1)
        near_copy(1).start()
        take_near(0)
        near_copy(1).wait_send()


def per_device(n_sub, n_dom, a_cols, a_blocks, p_blocks, send_rows):
    rows, per_row = a_cols.shape
    size = p_blocks.shape[1]
    items = rows * per_row
    table_rows = (items + 8) // 8 * 8
    block = (size, size)
    dma = pltpu.SemaphoreType.DMA
    operands = (a_cols, send_rows.reshape(-1), a_blocks, p_blocks)
    return pl.pallas_call(
        functools.partial(kernel, n_sub, n_dom, rows, per_row, size),
        out_shape=jax.ShapeDtypeStruct((1, size, (n_dom + 2) * size), BF16),
        in_specs=[pl.BlockSpec(memory_space=pltpu.HBM)] * 4,
        out_specs=pl.BlockSpec(memory_space=pltpu.VMEM),
        scratch_shapes=[
            pltpu.SMEM(operands[0].shape, jnp.int32),
            pltpu.SMEM(operands[1].shape, jnp.int32),
            pltpu.VMEM((rows, per_row) + block, BF16),
            pltpu.VMEM((rows,) + block, BF16),
            pltpu.VMEM((n_dom,) + block, BF16),
            pltpu.VMEM((n_dom,) + block, BF16),
            pltpu.VMEM((2, rows) + block, BF16),
            pltpu.VMEM((items + 1,) + block, F32),
            pltpu.VMEM((3 * rows + n_dom, size, 2 * size), BF16),
            pltpu.VMEM((table_rows, 128), jnp.int32),
            pltpu.SMEM((table_rows, 128), jnp.int32),
            dma, dma, dma, dma, dma,
            dma((2,)), dma((long_side_of(n_dom) + 1,)), dma((2,)), dma((2,)), pltpu.SemaphoreType.REGULAR,
        ],
        compiler_params=pltpu.CompilerParams(
            collective_id=0, has_side_effects=True, vmem_limit_bytes=48 * 1024 * 1024
        ),
        cost_estimate=pl.CostEstimate(
            flops=2 * (items + 2 * codes_of(rows, n_dom)) * size**3,
            bytes_accessed=2 * size * size * (items + rows + n_dom + 2),
            transcendentals=0,
        ),
    )(*(pltpu.with_memory_space_constraint(x, pltpu.HBM) for x in operands))


def codes_of(rows, n_dom):
    return 3 * rows + n_dom


def solution(mesh):
    placed = (
        P(("sub", "dom"), None),
        P(("sub", "dom"), None, None, None),
        P(("sub", "dom"), None, None),
        P(("sub", "dom"), None),
    )
    return jax.shard_map(
        functools.partial(per_device, mesh.shape["sub"], mesh.shape["dom"]),
        mesh=mesh,
        in_specs=placed,
        out_specs=P(("sub", "dom"), None, None),
        check_vma=False,
    )
```
